256 devices in a mesh: rep: 32 (over z_lo, x, core), fsdp: 8 (over z_hi, y).
Axes of the slice: x: 4, y: 4, z: 8 (z_hi: 2, z_lo: 4; z = z_hi * 4 + z_lo), core: 2. Of those that a mesh axis runs over, the one named last changes fastest.
Arguments:
- local_params: float32 [32, 256, 8192], P('rep', 'fsdp'), may hold values from -6 to 6
- global_params: float32 [256, 8192], P('fsdp'), may hold values from -6 to 6
- momentum: float32 [256, 8192], P('fsdp', 'rep'), may hold values from -3 to 3
- tokens: bfloat16 [16384, 8192], P('rep', 'fsdp'), may hold values from -0.29882812 to 0.29882812
- kv_weight: bfloat16 [32, 8192, 2048], P('rep', 'fsdp'), may hold values from -0.5 to 0.5
- kv_cotangent: bfloat16 [16384, 2048], P(('rep', 'fsdp')), may hold values from -1.5 to 1.5
Outputs:
- new_global: float32 [256, 8192], P('fsdp', 'rep')
- new_momentum: float32 [256, 8192], P('fsdp', 'rep')
- mixed_local: float32 [32, 256, 8192], P('rep', 'fsdp')
- kv_out: float32 [16384, 2048], P(('rep', 'fsdp'))
- grad_weight: bfloat16 [32, 8192, 2048], P('rep', 'fsdp')
- grad_tokens: float32 [16384, 8192], P('rep', 'fsdp')
The draws below stay inside these ranges and needn't reach their ends.
All inputs are finite; a program needn't handle non-finite values. Where the reference program divides by a largest or mean magnitude, that divisor is 1e-20 or more.
Results may differ from the reference program's by a relative error of at most 0.014.
Values may be sent and summed in bfloat16 or wider, within the bound.
No kernel may reach another device: no remote copies, remote signals or barrier semaphores. Data moves between devices by JAX's collectives and lax.ppermute only.
A program may use at most 64 MiB of HBM per device.

```python
import jax
import jax.numpy as jnp
from jax import lax

D = 8192
KV = 2048
BLOCK = 64
TOK_REP = 512
ROWS = 256
REPS = 32
TOKENS = 16384
N_REP = 32
N_FSDP = 8


def block_levels(key, extent, shards, smallest, largest):
    factor_of = 1.0
    for position, shards_of in shards:
        draws = jax.random.uniform(jax.random.fold_in(jax.random.fold_in(key, 6), position), (shards_of,), jnp.float32, smallest / len(shards), largest / len(shards))
        factor_of = factor_of * jnp.repeat(jnp.exp(draws), extent[position] // shards_of).reshape((-1,) + (1,) * (len(extent) - 1 - position))
    return factor_of


def noise(key, dims, width, bound, cuts=(), dtype=jnp.bfloat16):
    values = width * jax.random.normal(key, dims, jnp.float32)
    if cuts:
        values = values * block_levels(key, dims, cuts, -0.22, 0.18)
    return jnp.clip(values, -bound, bound).astype(dtype)


def setup_inputs(seed: int = 0) -> dict:
    keys = jax.random.split(jax.random.key(seed), 7)
    local_params = noise(keys[0], (REPS, ROWS, D), 1.0, 6.0, ((0, 32), (1, 8)), jnp.float32)
    global_params = noise(keys[1], (ROWS, D), 1.0, 6.0, ((0, 8),), jnp.float32)
    momentum = noise(keys[2], (ROWS, D), 0.5, 3.0, ((0, 8), (1, 32)), jnp.float32)
    tokens = noise(keys[3], (TOKENS, D), 0.05, 0.29882812, ((0, 32), (1, 8)))
    kv_weight = noise(keys[4], (REPS, D, KV), (KV // 16) ** -0.5, 0.5, ((0, 32), (1, 8)))
    kv_cotangent = noise(keys[5], (TOKENS, KV), 0.25, 1.5, ((0, 256),))
    return {"local_params": local_params, "global_params": global_params, "momentum": momentum, "tokens": tokens, "kv_weight": kv_weight, "kv_cotangent": kv_cotangent}


epsilon = 1e-6
momentum_rate = 0.9
outer_rate = 0.7
mix_rate = 0.5


def inner_step(operands):
    token_rows, weight_rows, cot_rows = operands
    grouped = token_rows.astype(jnp.float32).reshape(TOK_REP, N_FSDP, D // N_FSDP)
    weight_groups = weight_rows.astype(jnp.float32).reshape(N_FSDP, D // N_FSDP, KV)
    partial_value = jnp.einsum('tfd,fdk->ftk', grouped, weight_groups)
    partial_value = lax.optimization_barrier(partial_value.astype(jnp.bfloat16))
    kv_rows = jnp.sum(partial_value.astype(jnp.float32), axis=0)
    grad_w = jnp.dot(token_rows.T, cot_rows, preferred_element_type=jnp.float32).astype(jnp.bfloat16)
    grad_x = jnp.dot(cot_rows, weight_rows.T, preferred_element_type=jnp.float32)
    return kv_rows, grad_w, grad_x


def reference(local_params, global_params, momentum, tokens, kv_weight, kv_cotangent):
    pseudo = global_params[None] - local_params
    blocked = pseudo.reshape(N_REP, ROWS, D // BLOCK, BLOCK)
    scales = (jnp.max(jnp.abs(blocked), axis=-1) + epsilon).astype(jnp.bfloat16)
    quantized = (blocked / scales[..., None].astype(jnp.float32)).astype(jnp.bfloat16)
    restored = quantized.astype(jnp.float32) * scales[..., None].astype(jnp.float32)
    delta_sum = jnp.sum(restored, axis=0).reshape(ROWS, D)
    delta = delta_sum / N_REP
    new_momentum = momentum_rate * momentum + delta
    new_global = global_params - outer_rate * (delta + momentum_rate * new_momentum)
    mixed_local = mix_rate * local_params + (1.0 - mix_rate) * new_global[None]
    kv_rows, grad_weight, grad_x = lax.map(inner_step, (tokens.reshape(N_REP, TOK_REP, D), kv_weight, kv_cotangent.reshape(N_REP, TOK_REP, KV)))
    kv_out = kv_rows.reshape(N_REP * TOK_REP, KV)
    grad_tokens = grad_x.reshape(N_REP * TOK_REP, D)
    return new_global, new_momentum, mixed_local, kv_out, grad_weight, grad_tokens
```

```python
import jax
import jax.numpy as jnp
from jax import lax
from jax.experimental import pallas as pl
from jax.experimental.pallas import tpu as pltpu
from jax.sharding import PartitionSpec as P

BLOCK = 64
epsilon = 1e-06
momentum_rate = 0.9
outer_rate = 0.7
mix_rate = 0.5

N_REP = 32
N_FSDP = 8
OWN = 256
ROWS = 32
MASKS = (0, 3, 1, 2)

f32 = jnp.float32
bf16 = jnp.bfloat16


def swap_rep(value, mask):
    return lax.ppermute(value, "rep", [(r, r ^ mask) for r in range(N_REP)])


def swap_z(value):
    return lax.ppermute(value, "fsdp", [(f, f ^ 4) for f in range(N_FSDP)])


def shift_y(value, step):
    return lax.ppermute(
        value, "fsdp", [(f, (f & 4) | ((f + step) & 3)) for f in range(N_FSDP)]
    )


def column_of(rep, position, z_lo, core):
    x = ((rep >> 1) & 3) ^ MASKS[position]
    return pl.multiple_of((z_lo * 8 + x * 2 + core) * OWN, OWN)


def quantize_kernel(rep_ref, local_ref, global_ref, keep_ref, send_ref):
    rep = rep_ref[0]
    low = lax.broadcasted_iota(jnp.int32, (ROWS, 128), 1) < BLOCK

    def restored(column):
        parts = []
        for half in range(2):
            at = pl.ds(column + half * 128, 128)
            pseudo = global_ref[:, at] - local_ref[0, :, at]
            size = jnp.abs(pseudo)
            first = jnp.max(jnp.where(low, size, 0.0), axis=1, keepdims=True)
            second = jnp.max(jnp.where(low, 0.0, size), axis=1, keepdims=True)
            scale = (jnp.where(low, first, second) + epsilon).astype(bf16).astype(f32)
            parts.append((pseudo / scale).astype(bf16).astype(f32) * scale)
        return jnp.concatenate(parts, axis=1)

    core = rep & 1
    for position in range(4):
        for z_lo in range(4):
            send_ref[position, z_lo] = restored(
                column_of(rep, position, z_lo, 1 - core)
            ).astype(bf16)
            keep_ref[position, z_lo] = restored(column_of(rep, position, z_lo, core))


VMEM = pl.BlockSpec(memory_space=pltpu.VMEM)
SMEM = pl.BlockSpec(memory_space=pltpu.SMEM)


def quantize(rep, local_params, global_params):
    return pl.pallas_call(
        quantize_kernel,
        out_shape=(
            jax.ShapeDtypeStruct((4, 4, ROWS, OWN), f32),
            jax.ShapeDtypeStruct((4, 4, ROWS, OWN), bf16),
        ),
        in_specs=[SMEM, VMEM, VMEM],
        out_specs=(VMEM, VMEM),
        compiler_params=pltpu.CompilerParams(vmem_limit_bytes=16 * 2**20),
        name="quantize",
    )(rep, local_params, global_params)


def mix_kernel(rep_ref, local_ref, global_ref, own_ref, other_ref, mixed_ref):
    rep = rep_ref[0]
    core = rep & 1
    for position in range(4):
        for z_lo in range(4):
            for update_ref, whose in ((own_ref, core), (other_ref, 1 - core)):
                at = pl.ds(column_of(rep, position, z_lo, whose), OWN)
                new_global = global_ref[:, at] - update_ref[position, z_lo].astype(f32)
                mixed_ref[0, :, at] = (
                    mix_rate * local_ref[0, :, at] + (1.0 - mix_rate) * new_global
                )


def mix(rep, local_params, global_params, own, other):
    return pl.pallas_call(
        mix_kernel,
        out_shape=jax.ShapeDtypeStruct(local_params.shape, f32),
        in_specs=[SMEM, VMEM, VMEM, VMEM, VMEM],
        out_specs=VMEM,
        compiler_params=pltpu.CompilerParams(vmem_limit_bytes=16 * 2**20),
        name="mix",
    )(rep, local_params, global_params, own, other)


def outer_step(rep, local_params, global_params, momentum):
    keep, send = quantize(rep.reshape(1), local_params, global_params)
    total = keep + swap_rep(send, 1).astype(f32)
    got = swap_rep(total[2:].astype(bf16), 2)
    total = total[:2] + got.astype(f32)
    got = swap_rep(total[1].astype(bf16), 6)
    total = total[0] + got.astype(f32)
    z_lo = rep >> 3
    mine = momentum.astype(bf16)[None]
    got = swap_rep(jnp.concatenate([total.astype(bf16), mine]), 8)
    total = total + got[:4].astype(f32)
    pair = jnp.concatenate([mine, got[4:]])
    got = swap_rep(jnp.concatenate([total.astype(bf16), pair]), 16)
    total = total + got[:4].astype(f32)
    momenta = jnp.concatenate([pair, got[4:]]).astype(f32)
    delta = total / N_REP
    own_delta = lax.dynamic_index_in_dim(delta, z_lo, 0, keepdims=False)
    new_momentum = momentum_rate * momentum + own_delta
    own_global = lax.dynamic_slice_in_dim(global_params, rep * OWN, OWN, 1)
    new_global = own_global - outer_rate * (own_delta + momentum_rate * new_momentum)
    momenta = jnp.stack(
        [
            lax.dynamic_index_in_dim(momenta, z_lo ^ z, 0, keepdims=False)
            for z in range(4)
        ]
    )
    update = outer_rate * (
        delta + momentum_rate * (momentum_rate * momenta + delta)
    )
    update = update.astype(bf16)[None]
    update = jnp.concatenate([update, swap_rep(update, 6)])
    update = jnp.concatenate([update, swap_rep(update, 2)])
    other = swap_rep(update, 1)
    mixed = mix(rep.reshape(1), local_params, global_params, update, other)
    return new_global, new_momentum, mixed


def rows_of(value, target_y, z_hi):
    return lax.dynamic_slice_in_dim(value, z_hi * 256 + target_y * 64, 64, 0)


def project(fsdp, tokens, weight):
    y, z_hi = fsdp & 3, fsdp >> 2
    partial = jnp.dot(tokens, weight, preferred_element_type=f32).astype(bf16)
    chunk = [
        [rows_of(partial, (y + d) & 3, z) for z in range(2)] for d in range(4)
    ]
    from_below = shift_y(chunk[2][0], 1)
    from_above = shift_y(chunk[2][1], -1)
    up = jnp.concatenate(
        [(chunk[1][0].astype(f32) + from_below.astype(f32)).astype(bf16), chunk[1][1]]
    )
    down = jnp.concatenate(
        [chunk[3][0], (chunk[3][1].astype(f32) + from_above.astype(f32)).astype(bf16)]
    )
    from_below = shift_y(up, 1).astype(f32)
    from_above = shift_y(down, -1).astype(f32)
    total = (
        jnp.concatenate([chunk[0][0], chunk[0][1]]).astype(f32) + from_below + from_above
    )
    mine = lax.dynamic_slice_in_dim(total, z_hi * 64, 64, 0)
    theirs = lax.dynamic_slice_in_dim(total, 64 - z_hi * 64, 64, 0)
    return mine + swap_z(theirs.astype(bf16)).astype(f32)


def gather_y(own):
    below = shift_y(own, 1)
    above = shift_y(own, -1)
    far = jnp.concatenate([shift_y(below[:32], 1), shift_y(above[32:], -1)])
    return [own, above, far, below]


def shards(local_params, global_params, momentum, tokens, kv_weight, kv_cotangent):
    rep = lax.axis_index("rep")
    fsdp = lax.axis_index("fsdp")
    y, z_hi = fsdp & 3, fsdp >> 2
    weight = kv_weight[0]

    near = gather_y(kv_cotangent)
    far = gather_y(swap_z(kv_cotangent))
    kv_out = project(fsdp, tokens, weight)
    cotangent = jnp.zeros((512, 2048), bf16)
    for z, pieces in ((z_hi, near), (1 - z_hi, far)):
        for d, piece in enumerate(pieces):
            cotangent = lax.dynamic_update_slice_in_dim(
                cotangent, piece, z * 256 + ((y + d) & 3) * 64, 0
            )
    grad_weight = lax.dot_general(
        tokens, cotangent, (((0,), (0,)), ((), ())), preferred_element_type=f32
    ).astype(bf16)[None]
    grad_tokens = lax.dot_general(
        cotangent, weight, (((1,), (1,)), ((), ())), preferred_element_type=f32
    )
    new_global, new_momentum, mixed = outer_step(
        rep, local_params, global_params, momentum
    )
    return new_global, new_momentum, mixed, kv_out, grad_weight, grad_tokens


def solution(mesh):
    return jax.shard_map(
        shards,
        mesh=mesh,
        in_specs=(
            P("rep", "fsdp", None),
            P("fsdp", None),
            P("fsdp", "rep"),
            P("rep", "fsdp"),
            P("rep", "fsdp", None),
            P(("rep", "fsdp"), None),
        ),
        out_specs=(
            P("fsdp", "rep"),
            P("fsdp", "rep"),
            P("rep", "fsdp", None),
            P(("rep", "fsdp"), None),
            P("rep", "fsdp", None),
            P("rep", "fsdp"),
        ),
        check_vma=False,
    )
```

```python
import jax
import jax.numpy as jnp
from jax import lax
from jax.experimental import pallas as pl
from jax.experimental.pallas import tpu as pltpu
from jax.sharding import PartitionSpec as P

BLOCK = 64
epsilon = 1e-06
momentum_rate = 0.9
outer_rate = 0.7
mix_rate = 0.5

N_REP = 32
N_FSDP = 8
OWN = 256
ROWS = 32
MASKS = (0, 3, 1, 2)

f32 = jnp.float32
bf16 = jnp.bfloat16
VMEM = pl.BlockSpec(memory_space=pltpu.VMEM)
SMEM = pl.BlockSpec(memory_space=pltpu.SMEM)
HBM = pl.BlockSpec(memory_space=pltpu.HBM)
NT = (((1,), (1,)), ((), ()))


def after(value, *others):
    return lax.optimization_barrier((value, *others))[0]


def swap_rep(value, mask):
    return lax.ppermute(value, "rep", [(r, r ^ mask) for r in range(N_REP)])


def swap_z(value):
    return lax.ppermute(value, "fsdp", [(f, f ^ 4) for f in range(N_FSDP)])


def shift_y(value, step):
    return lax.ppermute(
        value, "fsdp", [(f, (f & 4) | ((f + step) & 3)) for f in range(N_FSDP)]
    )


def call(kernel, outs, operands, limit=4, in_specs=None, out_specs=None, **more):
    return pl.pallas_call(
        kernel,
        out_shape=tuple(jax.ShapeDtypeStruct(*out) for out in outs),
        in_specs=in_specs or [VMEM] * len(operands),
        out_specs=out_specs or tuple(VMEM for _ in outs),
        cost_estimate=pl.CostEstimate(flops=0, bytes_accessed=0, transcendentals=0),
        compiler_params=pltpu.CompilerParams(vmem_limit_bytes=limit * 2**20),
        name=kernel.__name__,
        **more,
    )(*operands)


BEGIN_MB, GRADIENTS_MB, MIX_MB = 51, 51, 51


def column_of(rep, position, z_lo, core):
    x = ((rep >> 1) & 3) ^ MASKS[position]
    return pl.multiple_of((z_lo * 8 + x * 2 + core) * OWN, OWN)


def restored(pseudo):
    low = lax.broadcasted_iota(jnp.int32, pseudo.shape, 1) < BLOCK
    size = jnp.abs(pseudo)
    first = jnp.max(jnp.where(low, size, 0.0), axis=1, keepdims=True)
    second = jnp.max(jnp.where(low, 0.0, size), axis=1, keepdims=True)
    scale = (jnp.where(low, first, second) + epsilon).astype(bf16).astype(f32)
    return (pseudo / scale).astype(bf16).astype(f32) * scale


def begin(
    rep_ref, fsdp_ref, local_hbm, global_hbm, tokens_hbm, weight_hbm,
    keep, send, own_global, far, up, down, own,
    local, globals_, ordered, weight, fragment_sems, token_sems, weight_sem,
):
    rep, fsdp = rep_ref[0], fsdp_ref[0]
    core = rep & 1
    outs = ((2, far), (1, up), (3, down), (0, own))
    fragment = []
    for part in range(2):
        at = pl.ds(part * 16, 16)
        fragment.append(
            (
                pltpu.make_async_copy(
                    local_hbm.at[0, at], local.at[at], fragment_sems.at[0, part]
                ),
                pltpu.make_async_copy(
                    global_hbm.at[at], globals_.at[at], fragment_sems.at[1, part]
                ),
            )
        )
    token_copies = []
    for i, (d, _) in enumerate(outs):
        for z in range(2):
            token_copies.append(
                pltpu.make_async_copy(
                    tokens_hbm.at[pl.ds(chunk_rows(fsdp, d, z), 64)],
                    ordered.at[pl.ds(i * 128 + z * 64, 64)],
                    token_sems.at[i * 2 + z],
                )
            )
    weight_copy = pltpu.make_async_copy(weight_hbm.at[0], weight, weight_sem)
    for copy in token_copies:
        copy.start()
    weight_copy.start()
    for pair in fragment:
        for copy in pair:
            copy.start()

    for copy in token_copies:
        copy.wait()
    weight_copy.wait()
    for tile in range(8):
        at = slice(tile * 256, tile * 256 + 256)
        partial = jnp.dot(ordered[...], weight[:, at], preferred_element_type=f32).astype(
            bf16
        )
        for i, (_, out) in enumerate(outs):
            out[:, at] = partial[i * 128 : i * 128 + 128]

    def pseudo(rows, column):
        at = pl.ds(column, 128)
        return restored(globals_[rows, at] - local[rows, at])

    for part, pair in enumerate(fragment):
        for copy in pair:
            copy.wait()
        rows = slice(part * 16, part * 16 + 16)
        for position in range(4):
            for z in range(4):
                for half in range(2):
                    to = slice(half * 128, half * 128 + 128)
                    send[position, z, rows, to] = pseudo(
                        rows, column_of(rep, position, z, 1 - core) + half * 128
                    ).astype(bf16)
                    keep[position, z, rows, to] = pseudo(
                        rows, column_of(rep, position, z, core) + half * 128
                    )
    own_global[...] = globals_[:, pl.ds(column_of(rep, 0, rep >> 3, core), OWN)]


def sum_core(keep, got, rest, send):
    rest[...] = keep[:2] + got[:2].astype(f32)
    send[...] = (keep[2:] + got[2:].astype(f32)).astype(bf16)


def sum_x_pair(keep, got, rest, send):
    rest[...] = keep[0] + got[0].astype(f32)
    send[...] = (keep[1] + got[1].astype(f32)).astype(bf16)


def sum_x(keep, got, momentum, rest, send):
    total = keep[...] + got[...].astype(f32)
    rest[...] = total
    send[:4] = total.astype(bf16)
    send[4] = momentum[...].astype(bf16)


def sum_z_pair(keep, got, momentum, rest, send):
    total = keep[...] + got[:4].astype(f32)
    rest[...] = total
    send[:4] = total.astype(bf16)
    send[4] = momentum[...].astype(bf16)
    send[5] = got[4]


def update_step(
    rep_ref, keep, near, far, momentum, own_global, new_global, new_momentum, update
):
    z_lo = rep_ref[0] >> 3

    def stepped(delta, moment):
        moment = momentum_rate * moment + delta
        return outer_rate * (delta + momentum_rate * moment), moment

    sources = (momentum, near.at[4], far.at[4], far.at[5])
    for mask, source in enumerate(sources):
        z = z_lo ^ mask
        delta = (keep[z] + far[z].astype(f32)) / N_REP
        change, moment = stepped(delta, source[...].astype(f32))
        update[z] = change.astype(bf16)
        if mask == 0:
            new_momentum[...] = moment
            new_global[...] = own_global[...] - change


def join(first, second, both):
    both[0] = first[...]
    both[1] = second[...]


def mix(
    rep_ref, local_hbm, global_hbm, own_near, own_far, other_near, other_far, mixed_hbm,
    local, globals_, mixed, sems,
):
    rep = rep_ref[0]
    core = rep & 1
    copies, results = [], []
    for part in range(4):
        at = pl.ds(part * 8, 8)
        copies.append(
            (
                pltpu.make_async_copy(local_hbm.at[0, at], local.at[at], sems.at[0, part]),
                pltpu.make_async_copy(global_hbm.at[at], globals_.at[at], sems.at[1, part]),
            )
        )
        results.append(
            pltpu.make_async_copy(mixed.at[at], mixed_hbm.at[0, at], sems.at[2, part])
        )
    for pair in copies:
        for copy in pair:
            copy.start()
    for part in range(4):
        for copy in copies[part]:
            copy.wait()
        rows = slice(part * 8, part * 8 + 8)
        for pieces, whose in (((own_near, own_far), core), ((other_near, other_far), 1 - core)):
            for position in range(4):
                for z in range(4):
                    at = pl.ds(column_of(rep, position, z, whose), OWN)
                    update = pieces[position // 2][position % 2, z, rows].astype(f32)
                    mixed[rows, at] = mix_rate * local[rows, at] + (1.0 - mix_rate) * (
                        globals_[rows, at] - update
                    )
        results[part].start()
    for copy in results:
        copy.wait()


def chunk_rows(fsdp, d, z):
    return pl.multiple_of(z * 256 + ((fsdp + d) & 3) * 64, 64)


def pack(far, below, above, up, down):
    up[:64] = far[:64]
    up[64:] = below[:32]
    down[:64] = far[64:]
    down[64:] = above[32:]


def add(up, down, from_below, from_above, up_out, down_out):
    up_out[:64] = (up[:64].astype(f32) + from_below[:64].astype(f32)).astype(bf16)
    up_out[64:] = up[64:]
    down_out[:64] = down[:64]
    down_out[64:] = (down[64:].astype(f32) + from_above[:64].astype(f32)).astype(bf16)


def fold(fsdp_ref, own, from_below, from_above, mine, theirs):
    z_hi = fsdp_ref[0] >> 2

    def total(z):
        at = pl.ds(pl.multiple_of(z * 64, 64), 64)
        return own[at].astype(f32) + from_below[at].astype(f32) + from_above[at].astype(f32)

    mine[...] = total(z_hi)
    theirs[...] = total(1 - z_hi).astype(bf16)


def gradients(
    fsdp_ref, tokens_hbm, weight_hbm, own, above, below, far_below, far_above,
    z_own, z_above, z_far, z_below, grad_weight_hbm, grad_tokens_hbm,
    rows, tokens, turned, weight, grad_weight, grad_tokens, in_sems, gx_sems, gw_sems,
):
    fsdp = fsdp_ref[0]
    z_hi = fsdp >> 2
    token_copy = pltpu.make_async_copy(tokens_hbm, tokens, in_sems.at[0])
    weight_copy = pltpu.make_async_copy(weight_hbm.at[0], weight, in_sems.at[1])
    token_copy.start()
    weight_copy.start()

    for d, part in ((0, own), (1, above), (3, below)):
        rows[pl.ds(chunk_rows(fsdp, d, z_hi), 64)] = part[...]
    first = chunk_rows(fsdp, 2, z_hi)
    rows[pl.ds(first, 32)] = far_below[64:]
    rows[pl.ds(pl.multiple_of(first + 32, 32), 32)] = far_above[64:]
    for d, part in enumerate((z_own, z_above, z_far, z_below)):
        rows[pl.ds(chunk_rows(fsdp, d, 1 - z_hi), 64)] = part[...]

    token_copy.wait()
    turned[...] = tokens[...].T
    results = []
    for tile in range(4):
        at = slice(tile * 256, tile * 256 + 256)
        grad_weight[at] = jnp.dot(
            turned[at], rows[...], preferred_element_type=f32
        ).astype(bf16)
        results.append(
            pltpu.make_async_copy(
                grad_weight.at[at], grad_weight_hbm.at[0, at], gw_sems.at[tile]
            )
        )
        results[-1].start()
    weight_copy.wait()
    for tile in range(2):
        at = slice(tile * 256, tile * 256 + 256)
        for part in range(4):
            to = slice(part * 256, part * 256 + 256)
            grad_tokens[at, to] = lax.dot_general(
                rows[at], weight[to], NT, preferred_element_type=f32
            )
        results.append(
            pltpu.make_async_copy(
                grad_tokens.at[at], grad_tokens_hbm.at[at], gx_sems.at[tile]
            )
        )
        results[-1].start()
    for copy in results:
        copy.wait()


def shards(local_params, global_params, momentum, tokens, kv_weight, kv_cotangent):
    rep = lax.axis_index("rep").reshape(1)
    fsdp = lax.axis_index("fsdp").reshape(1)
    part = ((128, 2048), bf16)
    block = (ROWS, OWN)

    z_own = swap_z(kv_cotangent)
    below = shift_y(kv_cotangent, 1)
    above = shift_y(kv_cotangent, -1)
    keep, send, own_global, far, up, down, own = call(
        begin,
        [((4, 4, *block), f32), ((4, 4, *block), bf16), (block, f32)] + [part] * 4,
        (rep, fsdp, local_params, global_params, tokens, kv_weight),
        BEGIN_MB,
        in_specs=[SMEM] * 2 + [HBM] * 4,
        scratch_shapes=[
            pltpu.VMEM((ROWS, 8192), f32),
            pltpu.VMEM((ROWS, 8192), f32),
            pltpu.VMEM((512, 1024), bf16),
            pltpu.VMEM((1024, 2048), bf16),
            pltpu.SemaphoreType.DMA((2, 2)),
            pltpu.SemaphoreType.DMA((8,)),
            pltpu.SemaphoreType.DMA(()),
        ],
    )
    got_core = swap_rep(send, 1)
    far_up, far_down = call(pack, [((96, 2048), bf16)] * 2, (far, below, above))
    from_below = shift_y(far_up, 1)
    from_above = shift_y(far_down, -1)


    rest, send = call(
        sum_core,
        [((2, 4, *block), f32), ((2, 4, *block), bf16)],
        (after(keep, far_up, z_own), got_core),
    )
    got = swap_rep(send, 2)
    up, down = call(add, [part] * 2, (after(up, got), down, from_below, from_above))
    sum_below = shift_y(up, 1)
    sum_above = shift_y(down, -1)
    rest, send = call(
        sum_x_pair,
        [((4, *block), f32), ((4, *block), bf16)],
        (after(rest, up), got),
    )
    got = swap_rep(send, 6)
    rest, send = call(
        sum_x,
        [((4, *block), f32), ((5, *block), bf16)],
        (after(rest, z_own), got, momentum),
    )
    near = swap_rep(send, 8)
    rest, send = call(
        sum_z_pair,
        [((4, *block), f32), ((6, *block), bf16)],
        (rest, near, momentum),
    )
    z_far = swap_rep(send, 16)

    z_own = after(z_own, near)
    z_pieces = (z_own, shift_y(z_own, -1), shift_y(z_own, 2), shift_y(z_own, 1))
    new_global, new_momentum, update = call(
        update_step,
        [(block, f32), (block, f32), ((4, *block), bf16)],
        (rep, rest, near, z_far, momentum, own_global),
        in_specs=[SMEM] + [VMEM] * 5,
    )
    mine, theirs = call(
        fold,
        [((64, 2048), f32), ((64, 2048), bf16)],
        (fsdp, after(own, update), sum_below, sum_above),
        in_specs=[SMEM, VMEM, VMEM, VMEM],
    )
    kv_out = mine + swap_z(theirs).astype(f32)
    (first,) = call(join, [((2, 4, *block), bf16)], (update, swap_rep(update, 6)))
    second = swap_rep(first, 2)
    (mixed,) = call(
        mix,
        [(local_params.shape, f32)],
        (rep, local_params, global_params, first, second, swap_rep(first, 1), swap_rep(second, 1)),
        MIX_MB,
        in_specs=[SMEM, HBM, HBM] + [VMEM] * 4,
        out_specs=(HBM,),
        scratch_shapes=[pltpu.VMEM((ROWS, 8192), f32)] * 3
        + [pltpu.SemaphoreType.DMA((3, 4))],
    )
    grad_weight, grad_tokens = call(
        gradients,
        [((1, 1024, 2048), bf16), ((512, 1024), f32)],
        (fsdp, tokens, kv_weight, after(kv_cotangent, first), above, below, from_below, from_above, *z_pieces),
        GRADIENTS_MB,
        in_specs=[SMEM, HBM, HBM] + [VMEM] * 9,
        out_specs=(HBM, HBM),
        scratch_shapes=[
            pltpu.VMEM((512, 2048), bf16),
            pltpu.VMEM((512, 1024), bf16),
            pltpu.VMEM((1024, 512), bf16),
            pltpu.VMEM((1024, 2048), bf16),
            pltpu.VMEM((1024, 2048), bf16),
            pltpu.VMEM((512, 1024), f32),
            pltpu.SemaphoreType.DMA((2,)),
            pltpu.SemaphoreType.DMA((2,)),
            pltpu.SemaphoreType.DMA((4,)),
        ],
    )
    return new_global, new_momentum, mixed, kv_out, grad_weight, grad_tokens


def solution(mesh):
    return jax.shard_map(
        shards,
        mesh=mesh,
        in_specs=(
            P("rep", "fsdp", None),
            P("fsdp", None),
            P("fsdp", "rep"),
            P("rep", "fsdp"),
            P("rep", "fsdp", None),
            P(("rep", "fsdp"), None),
        ),
        out_specs=(
            P("fsdp", "rep"),
            P("fsdp", "rep"),
            P("rep", "fsdp", None),
            P(("rep", "fsdp"), None),
            P("rep", "fsdp", None),
            P("rep", "fsdp"),
        ),
        check_vma=False,
    )
```

```python
import jax
import jax.numpy as jnp
from jax import lax
from jax.experimental import pallas as pl
from jax.experimental.pallas import tpu as pltpu
from jax.sharding import PartitionSpec as P

BLOCK = 64
epsilon = 1e-06
momentum_rate = 0.9
outer_rate = 0.7
mix_rate = 0.5

N_REP = 32
N_FSDP = 8
OWN = 256
ROWS = 32
MASKS = (0, 3, 1, 2)

f32 = jnp.float32
bf16 = jnp.bfloat16
VMEM = pl.BlockSpec(memory_space=pltpu.VMEM)
SMEM = pl.BlockSpec(memory_space=pltpu.SMEM)
HBM = pl.BlockSpec(memory_space=pltpu.HBM)
NT = (((1,), (1,)), ((), ()))


def after(value, *others):
    return lax.optimization_barrier((value, *others))[0]


def swap_rep(value, mask):
    return lax.ppermute(value, "rep", [(r, r ^ mask) for r in range(N_REP)])


def swap_z(value):
    return lax.ppermute(value, "fsdp", [(f, f ^ 4) for f in range(N_FSDP)])


def shift_y(value, step):
    return lax.ppermute(
        value, "fsdp", [(f, (f & 4) | ((f + step) & 3)) for f in range(N_FSDP)]
    )


def call(kernel, outs, operands, limit=4, in_specs=None, out_specs=None, **more):
    return pl.pallas_call(
        kernel,
        out_shape=tuple(jax.ShapeDtypeStruct(*out) for out in outs),
        in_specs=in_specs or [VMEM] * len(operands),
        out_specs=out_specs or tuple(VMEM for _ in outs),
        cost_estimate=pl.CostEstimate(flops=0, bytes_accessed=0, transcendentals=0),
        compiler_params=pltpu.CompilerParams(vmem_limit_bytes=limit * 2**20),
        name=kernel.__name__,
        **more,
    )(*operands)


BEGIN_MB, NEAR_MB, GRADIENTS_MB, MIX_MB = 50, 6, 12, 6


def column_of(rep, position, z_lo, core):
    x = ((rep >> 1) & 3) ^ MASKS[position]
    return pl.multiple_of((z_lo * 8 + x * 2 + core) * OWN, OWN)


def restored(pseudo):
    low = lax.broadcasted_iota(jnp.int32, pseudo.shape, 1) < BLOCK
    size = jnp.abs(pseudo)
    first = jnp.max(jnp.where(low, size, 0.0), axis=1, keepdims=True)
    second = jnp.max(jnp.where(low, 0.0, size), axis=1, keepdims=True)
    scale = (jnp.where(low, first, second) + epsilon).astype(bf16).astype(f32)
    return (pseudo / scale).astype(bf16).astype(f32) * scale


def begin(
    rep_ref, fsdp_ref, local_hbm, global_hbm, tokens_hbm, weight_hbm,
    keep, send, own_global, far, up, down, own, ordered,
    local, globals_, weight, fragment_sems, token_sems, weight_sems,
):
    rep, fsdp = rep_ref[0], fsdp_ref[0]
    core = rep & 1
    outs = (own, up, far, down)
    fragment = []
    for part in range(2):
        at = pl.ds(part * 16, 16)
        fragment.append(
            (
                pltpu.make_async_copy(
                    local_hbm.at[0, at], local.at[at], fragment_sems.at[0, part]
                ),
                pltpu.make_async_copy(
                    global_hbm.at[at], globals_.at[at], fragment_sems.at[1, part]
                ),
            )
        )
    token_copies = []
    for z in range(2):
        for d in range(4):
            i = z * 4 + d
            token_copies.append(
                pltpu.make_async_copy(
                    tokens_hbm.at[pl.ds(chunk_rows(fsdp, d, z), 64)],
                    ordered.at[pl.ds(i * 64, 64)],
                    token_sems.at[i],
                )
            )
    weight_copies = [
        pltpu.make_async_copy(
            weight_hbm.at[0, :, pl.ds(half * 1024, 1024)],
            weight.at[:, pl.ds(half * 1024, 1024)],
            weight_sems.at[half],
        )
        for half in range(2)
    ]
    for copy in token_copies + weight_copies:
        copy.start()
    for pair in fragment:
        for copy in pair:
            copy.start()

    for copy in token_copies:
        copy.wait()
    for tile in range(8):
        if tile % 4 == 0:
            weight_copies[tile // 4].wait()
        at = slice(tile * 256, tile * 256 + 256)
        partial = jnp.dot(ordered[...], weight[:, at], preferred_element_type=f32).astype(
            bf16
        )
        for d, out in enumerate(outs):
            out[:64, at] = partial[d * 64 : d * 64 + 64]
            out[64:, at] = partial[256 + d * 64 : 256 + d * 64 + 64]

    def pseudo(rows, column):
        at = pl.ds(column, 128)
        return restored(globals_[rows, at] - local[rows, at])

    for part, pair in enumerate(fragment):
        for copy in pair:
            copy.wait()
        rows = slice(part * 16, part * 16 + 16)
        for position in range(4):
            for z in range(4):
                for half in range(2):
                    to = slice(half * 128, half * 128 + 128)
                    send[position, z, rows, to] = pseudo(
                        rows, column_of(rep, position, z, 1 - core) + half * 128
                    ).astype(bf16)
                    keep[position, z, rows, to] = pseudo(
                        rows, column_of(rep, position, z, core) + half * 128
                    )
    own_global[...] = globals_[:, pl.ds(column_of(rep, 0, rep >> 3, core), OWN)]


def sum_core(keep, got, rest, send):
    rest[...] = keep[:2] + got[:2].astype(f32)
    send[...] = (keep[2:] + got[2:].astype(f32)).astype(bf16)


def sum_x_pair(keep, got, rest, send):
    rest[...] = keep[0] + got[0].astype(f32)
    send[...] = (keep[1] + got[1].astype(f32)).astype(bf16)


def sum_x(keep, got, momentum, rest, send):
    total = keep[...] + got[...].astype(f32)
    rest[...] = total
    send[:4] = total.astype(bf16)
    send[4] = momentum[...].astype(bf16)


def sum_z_pair(keep, got, momentum, rest, send):
    total = keep[...] + got[:4].astype(f32)
    rest[...] = total
    send[:4] = total.astype(bf16)
    send[4] = momentum[...].astype(bf16)
    send[5] = got[4]


def update_step(
    rep_ref, keep, near, far, momentum, own_global, new_global, new_momentum, update
):
    z_lo = rep_ref[0] >> 3

    def stepped(delta, moment):
        moment = momentum_rate * moment + delta
        return outer_rate * (delta + momentum_rate * moment), moment

    sources = (momentum, near.at[4], far.at[4], far.at[5])
    for mask, source in enumerate(sources):
        z = z_lo ^ mask
        delta = (keep[z] + far[z].astype(f32)) / N_REP
        change, moment = stepped(delta, source[...].astype(f32))
        update[z] = change.astype(bf16)
        if mask == 0:
            new_momentum[...] = moment
            new_global[...] = own_global[...] - change


def join(first, second, both):
    both[0] = first[...]
    both[1] = second[...]


def mix(
    rep_ref, local_hbm, global_hbm, own_near, own_far, other_near, other_far, mixed_hbm,
    local, globals_, mixed, sems,
):
    rep = rep_ref[0]
    core = rep & 1
    copies, results = [], []
    for part in range(4):
        at = pl.ds(part * 8, 8)
        copies.append(
            (
                pltpu.make_async_copy(local_hbm.at[0, at], local.at[at], sems.at[0, part]),
                pltpu.make_async_copy(global_hbm.at[at], globals_.at[at], sems.at[1, part]),
            )
        )
        results.append(
            pltpu.make_async_copy(mixed.at[at], mixed_hbm.at[0, at], sems.at[2, part])
        )
    for pair in copies:
        for copy in pair:
            copy.start()
    for part in range(4):
        for copy in copies[part]:
            copy.wait()
        rows = slice(part * 8, part * 8 + 8)
        for pieces, whose in (((own_near, own_far), core), ((other_near, other_far), 1 - core)):
            for position in range(4):
                for z in range(4):
                    at = pl.ds(column_of(rep, position, z, whose), OWN)
                    update = pieces[position // 2][position % 2, z, rows].astype(f32)
                    mixed[rows, at] = mix_rate * local[rows, at] + (1.0 - mix_rate) * (
                        globals_[rows, at] - update
                    )
        results[part].start()
    for copy in results:
        copy.wait()


def chunk_rows(fsdp, d, z):
    return pl.multiple_of(((fsdp >> 2) ^ z) * 256 + ((fsdp + d) & 3) * 64, 64)


def pack(far, below, above, up, down):
    up[:64] = far[:64]
    up[64:] = below[:32]
    down[:64] = far[64:]
    down[64:] = above[32:]


def add(up, down, from_below, from_above, up_out, down_out):
    up_out[:64] = (up[:64].astype(f32) + from_below[:64].astype(f32)).astype(bf16)
    up_out[64:] = up[64:]
    down_out[:64] = down[:64]
    down_out[64:] = (down[64:].astype(f32) + from_above[:64].astype(f32)).astype(bf16)


def fold(own, from_below, from_above, mine, theirs):
    total = own[...].astype(f32) + from_below[...].astype(f32) + from_above[...].astype(f32)
    mine[...] = total[:64]
    theirs[...] = total[64:].astype(bf16)


def near_rows(rows, own, above, below, far_below, far_above):
    for d, part in ((0, own), (1, above), (3, below)):
        rows[d * 64 : d * 64 + 64] = part[...]
    rows[128:160] = far_below[64:]
    rows[160:192] = far_above[64:]


def store_tokens(fsdp, source, grad_tokens_hbm, z, sems):
    copies = []
    for d in range(4):
        copies.append(
            pltpu.make_async_copy(
                source.at[pl.ds(d * 64, 64)],
                grad_tokens_hbm.at[pl.ds(chunk_rows(fsdp, d, z), 64)],
                sems.at[d],
            )
        )
        copies[-1].start()
    return copies


def near_gradients(
    fsdp_ref, tokens, weight, own, above, below, far_below, far_above,
    grad_tokens_hbm, turned, rows, tokens_near, sems,
):
    near_rows(rows, own, above, below, far_below, far_above)
    for tile in range(4):
        at = slice(tile * 256, tile * 256 + 256)
        tokens_near[:, at] = lax.dot_general(
            rows[...], weight[0, at], NT, preferred_element_type=f32
        )
    copies = store_tokens(fsdp_ref[0], tokens_near, grad_tokens_hbm, 0, sems)
    turned[...] = tokens[...].T
    for copy in copies:
        copy.wait()


def gradients(
    fsdp_ref, turned, weight, _, own, above, below, far_below, far_above,
    z_own, z_above, z_far, z_below, grad_weight_hbm, grad_tokens_hbm,
    rows, grad_weight, tokens_far, gw_sems, gx_sems,
):
    results = []
    for d, part in enumerate((z_own, z_above, z_far, z_below)):
        rows[256 + d * 64 : 256 + d * 64 + 64] = part[...]
    near_rows(rows, own, above, below, far_below, far_above)
    for tile in range(4):
        at = slice(tile * 256, tile * 256 + 256)
        grad_weight[at] = jnp.dot(
            turned[at], rows[...], preferred_element_type=f32
        ).astype(bf16)
        copy = pltpu.make_async_copy(
            grad_weight.at[at], grad_weight_hbm.at[0, at], gw_sems.at[tile]
        )
        copy.start()
        results.append(copy)
    for tile in range(4):
        at = slice(tile * 256, tile * 256 + 256)
        tokens_far[:, at] = lax.dot_general(
            rows[256:], weight[0, at], NT, preferred_element_type=f32
        )
    results += store_tokens(fsdp_ref[0], tokens_far, grad_tokens_hbm, 1, gx_sems)
    for copy in results:
        copy.wait()


def shards(local_params, global_params, momentum, tokens, kv_weight, kv_cotangent):
    rep = lax.axis_index("rep").reshape(1)
    fsdp = lax.axis_index("fsdp").reshape(1)
    part = ((128, 2048), bf16)
    block = (ROWS, OWN)

    z_own = swap_z(kv_cotangent)
    below = shift_y(kv_cotangent, 1)
    above = shift_y(kv_cotangent, -1)
    keep, send, own_global, far, up, down, own, ordered = call(
        begin,
        [((4, 4, *block), f32), ((4, 4, *block), bf16), (block, f32)] + [part] * 4
        + [((512, 1024), bf16)],
        (rep, fsdp, local_params, global_params, tokens, kv_weight),
        BEGIN_MB,
        in_specs=[SMEM] * 2 + [HBM] * 4,
        scratch_shapes=[
            pltpu.VMEM((ROWS, 8192), f32),
            pltpu.VMEM((ROWS, 8192), f32),
            pltpu.VMEM((1024, 2048), bf16),
            pltpu.SemaphoreType.DMA((2, 2)),
            pltpu.SemaphoreType.DMA((8,)),
            pltpu.SemaphoreType.DMA((2,)),
        ],
    )
    got_core = swap_rep(send, 1)
    far_up, far_down = call(pack, [((96, 2048), bf16)] * 2, (far, below, above))
    from_below = shift_y(far_up, 1)
    from_above = shift_y(far_down, -1)


    rest, send = call(
        sum_core,
        [((2, 4, *block), f32), ((2, 4, *block), bf16)],
        (after(keep, far_up, z_own), got_core),
    )
    got = swap_rep(send, 2)
    up, down = call(add, [part] * 2, (after(up, got), down, from_below, from_above))
    sum_below = shift_y(up, 1)
    sum_above = shift_y(down, -1)
    rest, send = call(
        sum_x_pair,
        [((4, *block), f32), ((4, *block), bf16)],
        (after(rest, up), got),
    )
    got = swap_rep(send, 6)
    grad_near, turned = call(
        near_gradients,
        [((512, 1024), f32), ((1024, 512), bf16)],
        (fsdp, ordered, kv_weight, after(kv_cotangent, send), above, below, from_below, from_above),
        NEAR_MB,
        in_specs=[SMEM] + [VMEM] * 7,
        out_specs=(HBM, VMEM),
        scratch_shapes=[
            pltpu.VMEM((256, 2048), bf16),
            pltpu.VMEM((256, 1024), f32),
            pltpu.SemaphoreType.DMA((4,)),
        ],
    )
    rest, send = call(
        sum_x,
        [((4, *block), f32), ((5, *block), bf16)],
        (after(rest, turned), got, momentum),
    )
    near = swap_rep(send, 8)
    rest, send = call(
        sum_z_pair,
        [((4, *block), f32), ((6, *block), bf16)],
        (rest, near, momentum),
    )
    z_far = swap_rep(send, 16)

    z_own = after(z_own, near)
    z_pieces = (z_own, shift_y(z_own, -1), shift_y(z_own, 2), shift_y(z_own, 1))
    mine, theirs = call(
        fold,
        [((64, 2048), f32), ((64, 2048), bf16)],
        (after(own, z_far), sum_below, sum_above),
    )
    new_global, new_momentum, update = call(
        update_step,
        [(block, f32), (block, f32), ((4, *block), bf16)],
        (rep, after(rest, theirs), near, z_far, momentum, own_global),
        in_specs=[SMEM] + [VMEM] * 5,
    )
    kv_out = mine + swap_z(theirs).astype(f32)
    (first,) = call(join, [((2, 4, *block), bf16)], (after(update, *z_pieces), swap_rep(update, 6)))
    second = swap_rep(first, 2)
    grad_weight, grad_tokens = call(
        gradients,
        [((1, 1024, 2048), bf16), ((512, 1024), f32)],
        (fsdp, turned, kv_weight, grad_near, after(kv_cotangent, first),
         above, below, from_below, from_above, *z_pieces),
        GRADIENTS_MB,
        in_specs=[SMEM, VMEM, VMEM, HBM] + [VMEM] * 9,
        out_specs=(HBM, HBM),
        input_output_aliases={3: 1},
        scratch_shapes=[
            pltpu.VMEM((512, 2048), bf16),
            pltpu.VMEM((1024, 2048), bf16),
            pltpu.VMEM((256, 1024), f32),
            pltpu.SemaphoreType.DMA((4,)),
            pltpu.SemaphoreType.DMA((4,)),
        ],
    )
    other_first = swap_rep(after(first, grad_weight), 1)
    other_second = swap_rep(after(second, grad_weight), 1)
    (mixed,) = call(
        mix,
        [(local_params.shape, f32)],
        (rep, local_params, global_params, first, second, other_first, other_second),
        MIX_MB,
        in_specs=[SMEM, HBM, HBM] + [VMEM] * 4,
        out_specs=(HBM,),
        scratch_shapes=[pltpu.VMEM((ROWS, 8192), f32)] * 3
        + [pltpu.SemaphoreType.DMA((3, 4))],
    )
    return new_global, new_momentum, mixed, kv_out, grad_weight, grad_tokens


def solution(mesh):
    return jax.shard_map(
        shards,
        mesh=mesh,
        in_specs=(
            P("rep", "fsdp", None),
            P("fsdp", None),
            P("fsdp", "rep"),
            P("rep", "fsdp"),
            P("rep", "fsdp", None),
            P(("rep", "fsdp"), None),
        ),
        out_specs=(
            P("fsdp", "rep"),
            P("fsdp", "rep"),
            P("rep", "fsdp", None),
            P(("rep", "fsdp"), None),
            P("rep", "fsdp", None),
            P("rep", "fsdp"),
        ),
        check_vma=False,
    )
```

```python
import jax
import jax.numpy as jnp
from jax import lax
from jax.experimental import pallas as pl
from jax.experimental.pallas import tpu as pltpu
from jax.sharding import PartitionSpec as P

BLOCK = 64
epsilon = 1e-06
momentum_rate = 0.9
outer_rate = 0.7
mix_rate = 0.5

N_REP = 32
N_FSDP = 8
OWN = 256
ROWS = 32
MASKS = (0, 3, 1, 2)

f32 = jnp.float32
bf16 = jnp.bfloat16
VMEM = pl.BlockSpec(memory_space=pltpu.VMEM)
SMEM = pl.BlockSpec(memory_space=pltpu.SMEM)
HBM = pl.BlockSpec(memory_space=pltpu.HBM)
NT = (((1,), (1,)), ((), ()))


def after(value, *others):
    return lax.optimization_barrier((value, *others))[0]


def swap_rep(value, mask):
    return lax.ppermute(value, "rep", [(r, r ^ mask) for r in range(N_REP)])


def swap_z(value):
    return lax.ppermute(value, "fsdp", [(f, f ^ 4) for f in range(N_FSDP)])


def shift_y(value, step):
    return lax.ppermute(
        value, "fsdp", [(f, (f & 4) | ((f + step) & 3)) for f in range(N_FSDP)]
    )


def call(kernel, outs, operands, limit=4, in_specs=None, out_specs=None, **more):
    return pl.pallas_call(
        kernel,
        out_shape=tuple(jax.ShapeDtypeStruct(*out) for out in outs),
        in_specs=in_specs or [VMEM] * len(operands),
        out_specs=out_specs or tuple(VMEM for _ in outs),
        cost_estimate=pl.CostEstimate(flops=0, bytes_accessed=0, transcendentals=0),
        compiler_params=pltpu.CompilerParams(vmem_limit_bytes=limit * 2**20),
        name=kernel.__name__,
        **more,
    )(*operands)


BEGIN_MB, NEAR_MB, GRADIENTS_MB, MIX_MB = 50, 6, 12, 6


def column_of(rep, position, z_lo, core):
    x = ((rep >> 1) & 3) ^ MASKS[position]
    return pl.multiple_of((z_lo * 8 + x * 2 + core) * OWN, OWN)


def restored(pseudo):
    low = lax.broadcasted_iota(jnp.int32, pseudo.shape, 1) < BLOCK
    size = jnp.abs(pseudo)
    first = jnp.max(jnp.where(low, size, 0.0), axis=1, keepdims=True)
    second = jnp.max(jnp.where(low, 0.0, size), axis=1, keepdims=True)
    scale = (jnp.where(low, first, second) + epsilon).astype(bf16).astype(f32)
    return (pseudo / scale).astype(bf16).astype(f32) * scale


def begin(
    rep_ref, fsdp_ref, local_hbm, global_hbm, tokens_hbm, weight_hbm,
    keep, send, own_global, far, up, down, own, ordered,
    local, globals_, weight, fragment_sems, token_sems, weight_sems,
):
    rep, fsdp = rep_ref[0], fsdp_ref[0]
    core = rep & 1
    outs = (own, up, far, down)
    fragment = []
    for part in range(2):
        at = pl.ds(part * 16, 16)
        fragment.append(
            (
                pltpu.make_async_copy(
                    local_hbm.at[0, at], local.at[at], fragment_sems.at[0, part]
                ),
                pltpu.make_async_copy(
                    global_hbm.at[at], globals_.at[at], fragment_sems.at[1, part]
                ),
            )
        )
    token_copies = []
    for z in range(2):
        for d in range(4):
            i = z * 4 + d
            token_copies.append(
                pltpu.make_async_copy(
                    tokens_hbm.at[pl.ds(chunk_rows(fsdp, d, z), 64)],
                    ordered.at[pl.ds(i * 64, 64)],
                    token_sems.at[i],
                )
            )
    weight_copies = [
        pltpu.make_async_copy(
            weight_hbm.at[0, :, pl.ds(half * 1024, 1024)],
            weight.at[:, pl.ds(half * 1024, 1024)],
            weight_sems.at[half],
        )
        for half in range(2)
    ]
    for copy in token_copies + weight_copies:
        copy.start()
    for pair in fragment:
        for copy in pair:
            copy.start()

    for copy in token_copies:
        copy.wait()
    for tile in range(8):
        if tile % 4 == 0:
            weight_copies[tile // 4].wait()
        at = slice(tile * 256, tile * 256 + 256)
        partial = jnp.dot(ordered[...], weight[:, at], preferred_element_type=f32).astype(
            bf16
        )
        for d, out in enumerate(outs):
            out[:64, at] = partial[d * 64 : d * 64 + 64]
            out[64:, at] = partial[256 + d * 64 : 256 + d * 64 + 64]

    def pseudo(rows, column):
        at = pl.ds(column, 128)
        return restored(globals_[rows, at] - local[rows, at])

    for part, pair in enumerate(fragment):
        for copy in pair:
            copy.wait()
        rows = slice(part * 16, part * 16 + 16)
        for position in range(4):
            for z in range(4):
                for half in range(2):
                    to = slice(half * 128, half * 128 + 128)
                    send[position, z, rows, to] = pseudo(
                        rows, column_of(rep, position, z, 1 - core) + half * 128
                    ).astype(bf16)
                    keep[position, z, rows, to] = pseudo(
                        rows, column_of(rep, position, z, core) + half * 128
                    )
    own_global[...] = globals_[:, pl.ds(column_of(rep, 0, rep >> 3, core), OWN)]


def sum_core(keep, got, rest, send):
    rest[...] = keep[:2] + got[:2].astype(f32)
    send[...] = (keep[2:] + got[2:].astype(f32)).astype(bf16)


def sum_x_pair(keep, got, rest, send):
    rest[...] = keep[0] + got[0].astype(f32)
    send[...] = (keep[1] + got[1].astype(f32)).astype(bf16)


def sum_x(keep, got, momentum, rest, send):
    total = keep[...] + got[...].astype(f32)
    rest[...] = total
    send[:4] = total.astype(bf16)
    send[4] = momentum[...].astype(bf16)


def sum_z_pair(keep, got, momentum, rest, send):
    total = keep[...] + got[:4].astype(f32)
    rest[...] = total
    send[:4] = total.astype(bf16)
    send[4] = momentum[...].astype(bf16)
    send[5] = got[4]


def update_step(
    rep_ref, keep, near, far, momentum, own_global, new_global, new_momentum, update
):
    z_lo = rep_ref[0] >> 3

    def stepped(delta, moment):
        moment = momentum_rate * moment + delta
        return outer_rate * (delta + momentum_rate * moment), moment

    sources = (momentum, near.at[4], far.at[4], far.at[5])
    for mask, source in enumerate(sources):
        z = z_lo ^ mask
        delta = (keep[z] + far[z].astype(f32)) / N_REP
        change, moment = stepped(delta, source[...].astype(f32))
        update[z] = change.astype(bf16)
        if mask == 0:
            new_momentum[...] = moment
            new_global[...] = own_global[...] - change


def join(first, second, both):
    both[0] = first[...]
    both[1] = second[...]


def mix(
    rep_ref, local_hbm, global_hbm, own_near, own_far, other_near, other_far, mixed_hbm,
    local, globals_, mixed, sems,
):
    rep = rep_ref[0]
    core = rep & 1
    copies, results = [], []
    for part in range(4):
        at = pl.ds(part * 8, 8)
        copies.append(
            (
                pltpu.make_async_copy(local_hbm.at[0, at], local.at[at], sems.at[0, part]),
                pltpu.make_async_copy(global_hbm.at[at], globals_.at[at], sems.at[1, part]),
            )
        )
        results.append(
            pltpu.make_async_copy(mixed.at[at], mixed_hbm.at[0, at], sems.at[2, part])
        )
    for pair in copies:
        for copy in pair:
            copy.start()
    for part in range(4):
        for copy in copies[part]:
            copy.wait()
        rows = slice(part * 8, part * 8 + 8)
        for pieces, whose in (((own_near, own_far), core), ((other_near, other_far), 1 - core)):
            for position in range(4):
                for z in range(4):
                    at = pl.ds(column_of(rep, position, z, whose), OWN)
                    update = pieces[position // 2][position % 2, z, rows].astype(f32)
                    mixed[rows, at] = mix_rate * local[rows, at] + (1.0 - mix_rate) * (
                        globals_[rows, at] - update
                    )
        results[part].start()
    for copy in results:
        copy.wait()


def chunk_rows(fsdp, d, z):
    return pl.multiple_of(((fsdp >> 2) ^ z) * 256 + ((fsdp + d) & 3) * 64, 64)


def pack(far, below, above, up, down):
    up[:64] = far[:64]
    up[64:] = below[:32]
    down[:64] = far[64:]
    down[64:] = above[32:]


def add(up, down, from_below, from_above, up_out, down_out):
    up_out[:64] = (up[:64].astype(f32) + from_below[:64].astype(f32)).astype(bf16)
    up_out[64:] = up[64:]
    down_out[:64] = down[:64]
    down_out[64:] = (down[64:].astype(f32) + from_above[:64].astype(f32)).astype(bf16)


def fold(own, from_below, from_above, mine, theirs):
    total = own[...].astype(f32) + from_below[...].astype(f32) + from_above[...].astype(f32)
    mine[...] = total[:64]
    theirs[...] = total[64:].astype(bf16)


def near_rows(rows, own, above, below, far_below, far_above):
    for d, part in ((0, own), (1, above), (3, below)):
        rows[d * 64 : d * 64 + 64] = part[...]
    rows[128:160] = far_below[64:]
    rows[160:192] = far_above[64:]


def store_tokens(fsdp, source, grad_tokens_hbm, z, sems):
    copies = []
    for d in range(4):
        copies.append(
            pltpu.make_async_copy(
                source.at[pl.ds(d * 64, 64)],
                grad_tokens_hbm.at[pl.ds(chunk_rows(fsdp, d, z), 64)],
                sems.at[d],
            )
        )
        copies[-1].start()
    return copies


def near_gradients(
    fsdp_ref, tokens, weight, own, above, below, far_below, far_above,
    grad_tokens_hbm, turned, rows, tokens_near, sems,
):
    near_rows(rows, own, above, below, far_below, far_above)
    for tile in range(4):
        at = slice(tile * 256, tile * 256 + 256)
        tokens_near[:, at] = lax.dot_general(
            rows[...], weight[0, at], NT, preferred_element_type=f32
        )
    copies = store_tokens(fsdp_ref[0], tokens_near, grad_tokens_hbm, 0, sems)
    turned[...] = tokens[...].T
    for copy in copies:
        copy.wait()


def gradients(
    fsdp_ref, turned, weight, _, own, above, below, far_below, far_above,
    z_own, z_above, z_far, z_below, grad_weight_hbm, grad_tokens_hbm,
    rows, grad_weight, tokens_far, gw_sems, gx_sems,
):
    results = []
    for d, part in enumerate((z_own, z_above, z_far, z_below)):
        rows[256 + d * 64 : 256 + d * 64 + 64] = part[...]
    near_rows(rows, own, above, below, far_below, far_above)
    for tile in range(4):
        at = slice(tile * 256, tile * 256 + 256)
        grad_weight[at] = jnp.dot(
            turned[at], rows[...], preferred_element_type=f32
        ).astype(bf16)
        copy = pltpu.make_async_copy(
            grad_weight.at[at], grad_weight_hbm.at[0, at], gw_sems.at[tile]
        )
        copy.start()
        results.append(copy)
    for tile in range(4):
        at = slice(tile * 256, tile * 256 + 256)
        tokens_far[:, at] = lax.dot_general(
            rows[256:], weight[0, at], NT, preferred_element_type=f32
        )
    results += store_tokens(fsdp_ref[0], tokens_far, grad_tokens_hbm, 1, gx_sems)
    for copy in results:
        copy.wait()


def shards(local_params, global_params, momentum, tokens, kv_weight, kv_cotangent):
    rep = lax.axis_index("rep").reshape(1)
    fsdp = lax.axis_index("fsdp").reshape(1)
    part = ((128, 2048), bf16)
    block = (ROWS, OWN)

    z_own = swap_z(kv_cotangent)
    below = shift_y(kv_cotangent, 1)
    above = shift_y(kv_cotangent, -1)
    keep, send, own_global, far, up, down, own, ordered = call(
        begin,
        [((4, 4, *block), f32), ((4, 4, *block), bf16), (block, f32)] + [part] * 4
        + [((512, 1024), bf16)],
        (rep, fsdp, local_params, global_params, tokens, kv_weight),
        BEGIN_MB,
        in_specs=[SMEM] * 2 + [HBM] * 4,
        scratch_shapes=[
            pltpu.VMEM((ROWS, 8192), f32),
            pltpu.VMEM((ROWS, 8192), f32),
            pltpu.VMEM((1024, 2048), bf16),
            pltpu.SemaphoreType.DMA((2, 2)),
            pltpu.SemaphoreType.DMA((8,)),
            pltpu.SemaphoreType.DMA((2,)),
        ],
    )
    got_core = swap_rep(send, 1)
    far_up, far_down = call(pack, [((96, 2048), bf16)] * 2, (far, below, above))
    from_below = shift_y(far_up, 1)
    from_above = shift_y(far_down, -1)


    rest, send = call(
        sum_core,
        [((2, 4, *block), f32), ((2, 4, *block), bf16)],
        (after(keep, far_up), got_core),
    )
    got = swap_rep(send, 2)
    up, down = call(add, [part] * 2, (after(up, got), down, from_below, from_above))
    sum_below = shift_y(up, 1)
    sum_above = shift_y(down, -1)
    rest, send = call(
        sum_x_pair,
        [((4, *block), f32), ((4, *block), bf16)],
        (after(rest, up), got),
    )
    got = swap_rep(send, 6)
    grad_near, turned = call(
        near_gradients,
        [((512, 1024), f32), ((1024, 512), bf16)],
        (fsdp, ordered, kv_weight, after(kv_cotangent, send, z_own), above, below, from_below, from_above),
        NEAR_MB,
        in_specs=[SMEM] + [VMEM] * 7,
        out_specs=(HBM, VMEM),
        scratch_shapes=[
            pltpu.VMEM((256, 2048), bf16),
            pltpu.VMEM((256, 1024), f32),
            pltpu.SemaphoreType.DMA((4,)),
        ],
    )
    rest, send = call(
        sum_x,
        [((4, *block), f32), ((5, *block), bf16)],
        (after(rest, turned), got, momentum),
    )
    near = swap_rep(send, 8)
    rest, send = call(
        sum_z_pair,
        [((4, *block), f32), ((6, *block), bf16)],
        (rest, near, momentum),
    )
    z_far = swap_rep(send, 16)

    z_own = after(z_own, near)
    z_pieces = (z_own, shift_y(z_own, -1), shift_y(z_own, 2), shift_y(z_own, 1))
    mine, theirs = call(
        fold,
        [((64, 2048), f32), ((64, 2048), bf16)],
        (after(own, z_far), sum_below, sum_above),
    )
    new_global, new_momentum, update = call(
        update_step,
        [(block, f32), (block, f32), ((4, *block), bf16)],
        (rep, after(rest, theirs), near, z_far, momentum, own_global),
        in_specs=[SMEM] + [VMEM] * 5,
    )
    kv_out = mine + swap_z(theirs).astype(f32)
    (first,) = call(join, [((2, 4, *block), bf16)], (after(update, *z_pieces), swap_rep(update, 6)))
    second = swap_rep(first, 2)
    grad_weight, grad_tokens = call(
        gradients,
        [((1, 1024, 2048), bf16), ((512, 1024), f32)],
        (fsdp, turned, kv_weight, grad_near, after(kv_cotangent, first),
         above, below, from_below, from_above, *z_pieces),
        GRADIENTS_MB,
        in_specs=[SMEM, VMEM, VMEM, HBM] + [VMEM] * 9,
        out_specs=(HBM, HBM),
        input_output_aliases={3: 1},
        scratch_shapes=[
            pltpu.VMEM((512, 2048), bf16),
            pltpu.VMEM((1024, 2048), bf16),
            pltpu.VMEM((256, 1024), f32),
            pltpu.SemaphoreType.DMA((4,)),
            pltpu.SemaphoreType.DMA((4,)),
        ],
    )
    other_first = swap_rep(after(first, grad_weight), 1)
    other_second = swap_rep(after(second, grad_weight), 1)
    (mixed,) = call(
        mix,
        [(local_params.shape, f32)],
        (rep, local_params, global_params, first, second, other_first, other_second),
        MIX_MB,
        in_specs=[SMEM, HBM, HBM] + [VMEM] * 4,
        out_specs=(HBM,),
        scratch_shapes=[pltpu.VMEM((ROWS, 8192), f32)] * 3
        + [pltpu.SemaphoreType.DMA((3, 4))],
    )
    return new_global, new_momentum, mixed, kv_out, grad_weight, grad_tokens


def solution(mesh):
    return jax.shard_map(
        shards,
        mesh=mesh,
        in_specs=(
            P("rep", "fsdp", None),
            P("fsdp", None),
            P("fsdp", "rep"),
            P("rep", "fsdp"),
            P("rep", "fsdp", None),
            P(("rep", "fsdp"), None),
        ),
        out_specs=(
            P("fsdp", "rep"),
            P("fsdp", "rep"),
            P("rep", "fsdp", None),
            P(("rep", "fsdp"), None),
            P("rep", "fsdp", None),
            P("rep", "fsdp"),
        ),
        check_vma=False,
    )
```

```python
import jax
import jax.numpy as jnp
from jax import lax
from jax.experimental import pallas as pl
from jax.experimental.pallas import tpu as pltpu
from jax.sharding import PartitionSpec as P

BLOCK = 64
epsilon = 1e-06
momentum_rate = 0.9
outer_rate = 0.7
mix_rate = 0.5

N_REP = 32
N_FSDP = 8
OWN = 256
ROWS = 32
MASKS = (0, 3, 1, 2)

f32 = jnp.float32
bf16 = jnp.bfloat16
VMEM = pl.BlockSpec(memory_space=pltpu.VMEM)
SMEM = pl.BlockSpec(memory_space=pltpu.SMEM)
HBM = pl.BlockSpec(memory_space=pltpu.HBM)
NT = (((1,), (1,)), ((), ()))


def after(value, *others):
    return lax.optimization_barrier((value, *others))[0]


def swap_rep(value, mask):
    return lax.ppermute(value, "rep", [(r, r ^ mask) for r in range(N_REP)])


def swap_z(value):
    return lax.ppermute(value, "fsdp", [(f, f ^ 4) for f in range(N_FSDP)])


def shift_y(value, step):
    return lax.ppermute(
        value, "fsdp", [(f, (f & 4) | ((f + step) & 3)) for f in range(N_FSDP)]
    )


def call(kernel, outs, operands, limit=4, in_specs=None, out_specs=None, **more):
    return pl.pallas_call(
        kernel,
        out_shape=tuple(jax.ShapeDtypeStruct(*out) for out in outs),
        in_specs=in_specs or [VMEM] * len(operands),
        out_specs=out_specs or tuple(VMEM for _ in outs),
        cost_estimate=pl.CostEstimate(flops=0, bytes_accessed=0, transcendentals=0),
        compiler_params=pltpu.CompilerParams(vmem_limit_bytes=limit * 2**20),
        name=kernel.__name__,
        **more,
    )(*operands)


BEGIN_MB, QUANTIZE_MB, NEAR_MB, GRADIENTS_MB, MIX_MB = 51, 50, 6, 12, 6


def column_of(rep, position, z_lo, core):
    x = ((rep >> 1) & 3) ^ MASKS[position]
    return pl.multiple_of((z_lo * 8 + x * 2 + core) * OWN, OWN)


def restored(pseudo):
    low = lax.broadcasted_iota(jnp.int32, pseudo.shape, 1) < BLOCK
    size = jnp.abs(pseudo)
    first = jnp.max(jnp.where(low, size, 0.0), axis=1, keepdims=True)
    second = jnp.max(jnp.where(low, 0.0, size), axis=1, keepdims=True)
    scale = (jnp.where(low, first, second) + epsilon).astype(bf16).astype(f32)
    return (pseudo / scale).astype(bf16).astype(f32) * scale


def project(
    fsdp_ref, tokens_hbm, weight_hbm, far, up, down, own, ordered,
    weight, token_sems, weight_sems,
):
    fsdp = fsdp_ref[0]
    outs = (own, up, far, down)
    token_copies = []
    for z in range(2):
        for d in range(4):
            i = z * 4 + d
            token_copies.append(
                pltpu.make_async_copy(
                    tokens_hbm.at[pl.ds(chunk_rows(fsdp, d, z), 64)],
                    ordered.at[pl.ds(i * 64, 64)],
                    token_sems.at[i],
                )
            )
    weight_copies = [
        pltpu.make_async_copy(
            weight_hbm.at[0, :, pl.ds(half * 1024, 1024)],
            weight.at[:, pl.ds(half * 1024, 1024)],
            weight_sems.at[half],
        )
        for half in range(2)
    ]
    for copy in token_copies + weight_copies:
        copy.start()

    for copy in token_copies:
        copy.wait()
    for tile in range(8):
        if tile % 4 == 0:
            weight_copies[tile // 4].wait()
        at = slice(tile * 256, tile * 256 + 256)
        partial = jnp.dot(ordered[...], weight[:, at], preferred_element_type=f32).astype(
            bf16
        )
        for d, out in enumerate(outs):
            out[:64, at] = partial[d * 64 : d * 64 + 64]
            out[64:, at] = partial[256 + d * 64 : 256 + d * 64 + 64]


def quantize(
    rep_ref, local_hbm, global_hbm, keep, send, own_global, local, globals_, fragment_sems
):
    rep = rep_ref[0]
    core = rep & 1
    fragment = []
    for part in range(2):
        at = pl.ds(part * 16, 16)
        fragment.append(
            (
                pltpu.make_async_copy(
                    local_hbm.at[0, at], local.at[at], fragment_sems.at[0, part]
                ),
                pltpu.make_async_copy(
                    global_hbm.at[at], globals_.at[at], fragment_sems.at[1, part]
                ),
            )
        )
    for pair in fragment:
        for copy in pair:
            copy.start()

    def pseudo(rows, column):
        at = pl.ds(column, 128)
        return restored(globals_[rows, at] - local[rows, at])

    for part, pair in enumerate(fragment):
        for copy in pair:
            copy.wait()
        rows = slice(part * 16, part * 16 + 16)
        for position in range(4):
            for z in range(4):
                for half in range(2):
                    to = slice(half * 128, half * 128 + 128)
                    send[position, z, rows, to] = pseudo(
                        rows, column_of(rep, position, z, 1 - core) + half * 128
                    ).astype(bf16)
                    keep[position, z, rows, to] = pseudo(
                        rows, column_of(rep, position, z, core) + half * 128
                    )
    own_global[...] = globals_[:, pl.ds(column_of(rep, 0, rep >> 3, core), OWN)]


def sum_core(keep, got, rest, send):
    rest[...] = keep[:2] + got[:2].astype(f32)
    send[...] = (keep[2:] + got[2:].astype(f32)).astype(bf16)


def sum_x_pair(keep, got, rest, send):
    rest[...] = keep[0] + got[0].astype(f32)
    send[...] = (keep[1] + got[1].astype(f32)).astype(bf16)


def sum_x(keep, got, momentum, rest, send):
    total = keep[...] + got[...].astype(f32)
    rest[...] = total
    send[:4] = total.astype(bf16)
    send[4] = momentum[...].astype(bf16)


def sum_z_pair(keep, got, momentum, rest, send):
    total = keep[...] + got[:4].astype(f32)
    rest[...] = total
    send[:4] = total.astype(bf16)
    send[4] = momentum[...].astype(bf16)
    send[5] = got[4]


def update_step(
    rep_ref, keep, near, far, momentum, own_global, new_global, new_momentum, update
):
    z_lo = rep_ref[0] >> 3

    def stepped(delta, moment):
        moment = momentum_rate * moment + delta
        return outer_rate * (delta + momentum_rate * moment), moment

    sources = (momentum, near.at[4], far.at[4], far.at[5])
    for mask, source in enumerate(sources):
        z = z_lo ^ mask
        delta = (keep[z] + far[z].astype(f32)) / N_REP
        change, moment = stepped(delta, source[...].astype(f32))
        update[z] = change.astype(bf16)
        if mask == 0:
            new_momentum[...] = moment
            new_global[...] = own_global[...] - change


def join(first, second, both):
    both[0] = first[...]
    both[1] = second[...]


def mix(
    rep_ref, local_hbm, global_hbm, own_near, own_far, other_near, other_far, mixed_hbm,
    local, globals_, mixed, sems,
):
    rep = rep_ref[0]
    core = rep & 1
    copies, results = [], []
    for part in range(4):
        at = pl.ds(part * 8, 8)
        copies.append(
            (
                pltpu.make_async_copy(local_hbm.at[0, at], local.at[at], sems.at[0, part]),
                pltpu.make_async_copy(global_hbm.at[at], globals_.at[at], sems.at[1, part]),
            )
        )
        results.append(
            pltpu.make_async_copy(mixed.at[at], mixed_hbm.at[0, at], sems.at[2, part])
        )
    for pair in copies:
        for copy in pair:
            copy.start()
    for part in range(4):
        for copy in copies[part]:
            copy.wait()
        rows = slice(part * 8, part * 8 + 8)
        for pieces, whose in (((own_near, own_far), core), ((other_near, other_far), 1 - core)):
            for position in range(4):
                for z in range(4):
                    at = pl.ds(column_of(rep, position, z, whose), OWN)
                    update = pieces[position // 2][position % 2, z, rows].astype(f32)
                    mixed[rows, at] = mix_rate * local[rows, at] + (1.0 - mix_rate) * (
                        globals_[rows, at] - update
                    )
        results[part].start()
    for copy in results:
        copy.wait()


def chunk_rows(fsdp, d, z):
    return pl.multiple_of(((fsdp >> 2) ^ z) * 256 + ((fsdp + d) & 3) * 64, 64)


def pack(far, below, above, up, down):
    up[:64] = far[:64]
    up[64:] = below[:32]
    down[:64] = far[64:]
    down[64:] = above[32:]


def add(up, down, from_below, from_above, up_out, down_out):
    up_out[:64] = (up[:64].astype(f32) + from_below[:64].astype(f32)).astype(bf16)
    up_out[64:] = up[64:]
    down_out[:64] = down[:64]
    down_out[64:] = (down[64:].astype(f32) + from_above[:64].astype(f32)).astype(bf16)


def fold(own, from_below, from_above, mine, theirs):
    total = own[...].astype(f32) + from_below[...].astype(f32) + from_above[...].astype(f32)
    mine[...] = total[:64]
    theirs[...] = total[64:].astype(bf16)


def near_rows(rows, own, above, below, far_below, far_above):
    for d, part in ((0, own), (1, above), (3, below)):
        rows[d * 64 : d * 64 + 64] = part[...]
    rows[128:160] = far_below[64:]
    rows[160:192] = far_above[64:]


def store_tokens(fsdp, source, grad_tokens_hbm, z, sems):
    copies = []
    for d in range(4):
        copies.append(
            pltpu.make_async_copy(
                source.at[pl.ds(d * 64, 64)],
                grad_tokens_hbm.at[pl.ds(chunk_rows(fsdp, d, z), 64)],
                sems.at[d],
            )
        )
        copies[-1].start()
    return copies


def near_gradients(
    fsdp_ref, tokens, weight, own, above, below, far_below, far_above,
    grad_tokens_hbm, turned, rows, tokens_near, sems,
):
    near_rows(rows, own, above, below, far_below, far_above)
    for tile in range(4):
        at = slice(tile * 256, tile * 256 + 256)
        tokens_near[:, at] = lax.dot_general(
            rows[...], weight[0, at], NT, preferred_element_type=f32
        )
    copies = store_tokens(fsdp_ref[0], tokens_near, grad_tokens_hbm, 0, sems)
    turned[...] = tokens[...].T
    for copy in copies:
        copy.wait()


def gradients(
    fsdp_ref, turned, weight, _, own, above, below, far_below, far_above,
    z_own, z_above, z_far, z_below, grad_weight_hbm, grad_tokens_hbm,
    rows, grad_weight, tokens_far, gw_sems, gx_sems,
):
    results = []
    for d, part in enumerate((z_own, z_above, z_far, z_below)):
        rows[256 + d * 64 : 256 + d * 64 + 64] = part[...]
    near_rows(rows, own, above, below, far_below, far_above)
    for tile in range(4):
        at = slice(tile * 256, tile * 256 + 256)
        tokens_far[:, at] = lax.dot_general(
            rows[256:], weight[0, at], NT, preferred_element_type=f32
        )
    results += store_tokens(fsdp_ref[0], tokens_far, grad_tokens_hbm, 1, gx_sems)
    for tile in range(8):
        at = slice(tile * 128, tile * 128 + 128)
        grad_weight[at] = jnp.dot(
            turned[at], rows[...], preferred_element_type=f32
        ).astype(bf16)
        copy = pltpu.make_async_copy(
            grad_weight.at[at], grad_weight_hbm.at[0, at], gw_sems.at[tile]
        )
        copy.start()
        results.append(copy)
    for copy in results:
        copy.wait()


def shards(local_params, global_params, momentum, tokens, kv_weight, kv_cotangent):
    rep = lax.axis_index("rep").reshape(1)
    fsdp = lax.axis_index("fsdp").reshape(1)
    part = ((128, 2048), bf16)
    block = (ROWS, OWN)

    z_own = swap_z(kv_cotangent)
    below = shift_y(kv_cotangent, 1)
    above = shift_y(kv_cotangent, -1)
    far, up, down, own, ordered = call(
        project,
        [part] * 4 + [((512, 1024), bf16)],
        (fsdp, tokens, kv_weight),
        BEGIN_MB,
        in_specs=[SMEM, HBM, HBM],
        scratch_shapes=[
            pltpu.VMEM((1024, 2048), bf16),
            pltpu.SemaphoreType.DMA((8,)),
            pltpu.SemaphoreType.DMA((2,)),
        ],
    )
    far_up, far_down = call(pack, [((96, 2048), bf16)] * 2, (far, below, above))
    from_below = shift_y(far_up, 1)
    from_above = shift_y(far_down, -1)


    keep, send, own_global = call(
        quantize,
        [((4, 4, *block), f32), ((4, 4, *block), bf16), (block, f32)],
        (after(rep, far), local_params, global_params),
        QUANTIZE_MB,
        in_specs=[SMEM, HBM, HBM],
        scratch_shapes=[
            pltpu.VMEM((ROWS, 8192), f32),
            pltpu.VMEM((ROWS, 8192), f32),
            pltpu.SemaphoreType.DMA((2, 2)),
        ],
    )
    got_core = swap_rep(send, 1)
    rest, send = call(
        sum_core,
        [((2, 4, *block), f32), ((2, 4, *block), bf16)],
        (after(keep, far_up), got_core),
    )
    got = swap_rep(send, 2)
    up, down = call(add, [part] * 2, (after(up, got), down, from_below, from_above))
    sum_below = shift_y(up, 1)
    sum_above = shift_y(down, -1)
    rest, send = call(
        sum_x_pair,
        [((4, *block), f32), ((4, *block), bf16)],
        (after(rest, up), got),
    )
    got = swap_rep(send, 6)
    grad_near, turned = call(
        near_gradients,
        [((512, 1024), f32), ((1024, 512), bf16)],
        (fsdp, ordered, kv_weight, after(kv_cotangent, send, z_own), above, below, from_below, from_above),
        NEAR_MB,
        in_specs=[SMEM] + [VMEM] * 7,
        out_specs=(HBM, VMEM),
        scratch_shapes=[
            pltpu.VMEM((256, 2048), bf16),
            pltpu.VMEM((256, 1024), f32),
            pltpu.SemaphoreType.DMA((4,)),
        ],
    )
    rest, send = call(
        sum_x,
        [((4, *block), f32), ((5, *block), bf16)],
        (after(rest, turned), got, momentum),
    )
    near = swap_rep(send, 8)
    rest, send = call(
        sum_z_pair,
        [((4, *block), f32), ((6, *block), bf16)],
        (rest, near, momentum),
    )
    z_far = swap_rep(send, 16)

    z_own = after(z_own, near)
    z_pieces = (z_own, shift_y(z_own, -1), shift_y(z_own, 2), shift_y(z_own, 1))
    mine, theirs = call(
        fold,
        [((64, 2048), f32), ((64, 2048), bf16)],
        (after(own, z_far), sum_below, sum_above),
    )
    new_global, new_momentum, update = call(
        update_step,
        [(block, f32), (block, f32), ((4, *block), bf16)],
        (rep, after(rest, theirs), near, z_far, momentum, own_global),
        in_specs=[SMEM] + [VMEM] * 5,
    )
    kv_out = mine + swap_z(theirs).astype(f32)
    (first,) = call(join, [((2, 4, *block), bf16)], (after(update, *z_pieces), swap_rep(update, 6)))
    second = swap_rep(first, 2)
    grad_weight, grad_tokens = call(
        gradients,
        [((1, 1024, 2048), bf16), ((512, 1024), f32)],
        (fsdp, turned, kv_weight, grad_near, after(kv_cotangent, first),
         above, below, from_below, from_above, *z_pieces),
        GRADIENTS_MB,
        in_specs=[SMEM, VMEM, VMEM, HBM] + [VMEM] * 9,
        out_specs=(HBM, HBM),
        input_output_aliases={3: 1},
        scratch_shapes=[
            pltpu.VMEM((512, 2048), bf16),
            pltpu.VMEM((1024, 2048), bf16),
            pltpu.VMEM((256, 1024), f32),
            pltpu.SemaphoreType.DMA((8,)),
            pltpu.SemaphoreType.DMA((4,)),
        ],
    )
    other_first = swap_rep(after(first, grad_weight), 1)
    other_second = swap_rep(after(second, grad_weight), 1)
    (mixed,) = call(
        mix,
        [(local_params.shape, f32)],
        (rep, local_params, global_params, first, second, other_first, other_second),
        MIX_MB,
        in_specs=[SMEM, HBM, HBM] + [VMEM] * 4,
        out_specs=(HBM,),
        scratch_shapes=[pltpu.VMEM((ROWS, 8192), f32)] * 3
        + [pltpu.SemaphoreType.DMA((3, 4))],
    )
    return new_global, new_momentum, mixed, kv_out, grad_weight, grad_tokens


def solution(mesh):
    return jax.shard_map(
        shards,
        mesh=mesh,
        in_specs=(
            P("rep", "fsdp", None),
            P("fsdp", None),
            P("fsdp", "rep"),
            P("rep", "fsdp"),
            P("rep", "fsdp", None),
            P(("rep", "fsdp"), None),
        ),
        out_specs=(
            P("fsdp", "rep"),
            P("fsdp", "rep"),
            P("rep", "fsdp", None),
            P(("rep", "fsdp"), None),
            P("rep", "fsdp", None),
            P("rep", "fsdp"),
        ),
        check_vma=False,
    )
```
